32 devices in a mesh: ctx: 16 (over z, x, core), head: 2 (over y).
Axes of the slice: x: 2, y: 2, z: 4, core: 2. Of those that a mesh axis runs over, the one named last changes fastest.
Arguments:
- queries: bfloat16 [6144, 4096], P('ctx', 'head'), may hold values from -8 to 8
- keys: bfloat16 [6144, 4096], P('ctx', 'head'), may hold values from -8 to 8
- values: bfloat16 [6144, 4096], P('ctx', 'head'), may hold values from -6 to 6
- rates: bfloat16 [6144, 8], P('ctx', 'head'), may hold values from 0.00025367737 to 0.0025482178
- fast_gate: bfloat16 [8, 512, 512], P('head'), may hold values from -0.25 to 0.25
- fast_up: bfloat16 [8, 512, 512], P('head'), may hold values from -0.25 to 0.25
- fast_down: bfloat16 [8, 512, 512], P('head'), may hold values from -0.25 to 0.25
Outputs:
- mixed: bfloat16 [6144, 4096], P('ctx', 'head')
The draws below stay inside these ranges and needn't reach their ends.
All inputs are finite; a program needn't handle non-finite values.
Results may differ from the reference program's by a relative error of at most 0.009.
Values may be sent and summed in bfloat16 or wider, within the bound.
A program may use at most 128 MiB of HBM per device.

```python
import math
import jax
import jax.numpy as jnp
from jax import lax

ATT_HEADS = 32
ATT_DIM = 128
FAST_HEADS = 8
FAST_DIM = 512
WINDOW = 1024
TOK_DEV = 384
D = 4096
TOKENS = 6144


def drawn_pair(key):
    base = jax.random.fold_in(key, 4099)
    first, second = jax.random.split(base, 2)
    shape = (TOKENS, ATT_HEADS * ATT_DIM)
    queries = jnp.clip(jax.random.normal(first, shape, jnp.float32), -6.0, 6.0)
    keys = jnp.clip(jax.random.normal(second, shape, jnp.float32), -6.0, 6.0)
    return (queries.astype(jnp.bfloat16), keys.astype(jnp.bfloat16))


def draw_queries(key, part):
    return drawn_pair(key)[0]


def draw_keys(key, part):
    return drawn_pair(key)[1]


def spiked(drawn, stream_key, source, target, shards_of, factor):
    def block_of(dim):
        return (jnp.arange(drawn.shape[dim]) // (drawn.shape[dim] // shards_of)).reshape((-1,) + (1,) * (drawn.ndim - 1 - dim))

    one_side = jax.random.permutation(stream_key, shards_of)[block_of(target)]
    other_side = (block_of(target) + shards_of // 2) % shards_of
    return jnp.where((block_of(source) == one_side) | (block_of(source) == other_side), factor * drawn, drawn)


def levels(stream_key, shape, cuts, smallest, top_value):
    gain = 1.0
    for dim, parts in cuts:
        draws = jax.random.uniform(jax.random.fold_in(jax.random.fold_in(stream_key, 6), dim), (parts,), jnp.float32, smallest / len(cuts), top_value / len(cuts))
        gain = gain * jnp.repeat(jnp.exp(draws), shape[dim] // parts).reshape((-1,) + (1,) * (len(shape) - 1 - dim))
    return gain


def gaussian(rng, extent, deviation, bound, cuts=(), held_as=jnp.bfloat16):
    array = jax.random.normal(rng, extent, jnp.float32) * deviation
    if len(cuts) > 0:
        array = levels(rng, extent, cuts, -0.22, 0.18) * array
    return jnp.clip(array, min=-bound, max=bound).astype(held_as)


def bell_draw_with(stream_key, dims, spread, reach, cuts, heavy, held_as=jnp.bfloat16):
    values = spread * jax.random.normal(stream_key, dims, jnp.float32)
    if cuts:
        values = values * levels(stream_key, dims, cuts, -0.22, 0.18)
    return jnp.clip(spiked(values, jax.random.fold_in(stream_key, 3), *heavy), -reach, reach).astype(held_as)


def setup_inputs(seed: int = 0) -> dict:
    key_list = jax.random.split(jax.random.key(seed), 8)
    return {
        "queries": draw_queries(jax.random.fold_in(key_list[7], 71), 0),
        "keys": draw_keys(jax.random.fold_in(key_list[7], 71), 0),
        "values": bell_draw_with(key_list[2], (TOKENS, D), 1.0, 6.0, ((0, 16), (1, 2)), (0, 1, 16, 2.0)),
        "rates": jnp.clip(jnp.exp(math.log(0.0025482178) - 2.3070862 * jax.random.uniform(key_list[3], (TOKENS, FAST_HEADS), jnp.float32) ** levels(key_list[3], (TOKENS, FAST_HEADS), ((0, 16), (1, 2)), -0.2, 0.2)), 0.00025367737, 0.0025482178).astype(jnp.bfloat16),
        "fast_gate": gaussian(key_list[4], (FAST_HEADS, FAST_DIM, FAST_DIM), FAST_DIM ** -0.5, 0.25, ((0, 2),)),
        "fast_up": gaussian(key_list[5], (FAST_HEADS, FAST_DIM, FAST_DIM), FAST_DIM ** -0.5, 0.25, ((0, 2),)),
        "fast_down": gaussian(key_list[6], (FAST_HEADS, FAST_DIM, FAST_DIM), FAST_DIM ** -0.5, 0.25, ((0, 2),)),
    }


def silu_parts(pre_act):
    sigmoid = jax.nn.sigmoid(pre_act)
    return (pre_act * sigmoid, sigmoid * (1.0 + pre_act * (1.0 - sigmoid)))

def fast_gradients(key_rows, value_rows, rate_column, gate, upward, downward):
    gate_pre = jnp.dot(key_rows, gate.T, preferred_element_type=jnp.float32)
    up_pre = jnp.dot(key_rows, upward.T, preferred_element_type=jnp.float32)
    activated, slope = silu_parts(gate_pre)
    hidden = (activated * up_pre).astype(jnp.bfloat16)
    out_grad = (-rate_column.astype(jnp.float32)[:, None] * value_rows.astype(jnp.float32)).astype(jnp.bfloat16)
    hidden_grad = jnp.dot(out_grad, downward, preferred_element_type=jnp.float32)
    gate_grad = (hidden_grad * up_pre * slope).astype(jnp.bfloat16)
    up_grad = (hidden_grad * activated).astype(jnp.bfloat16)
    grad_gate = jnp.dot(gate_grad.T, key_rows, preferred_element_type=jnp.float32)
    grad_up = jnp.dot(up_grad.T, key_rows, preferred_element_type=jnp.float32)
    grad_down = jnp.dot(out_grad.T, hidden, preferred_element_type=jnp.float32)
    return jnp.stack([grad_gate, grad_up, grad_down])

def renormalize(weights, gradient):
    initial = weights.astype(jnp.float32)
    moved = initial - gradient
    target = jnp.sqrt(lax.optimization_barrier(jnp.sum(initial * initial, axis=-1, keepdims=True)))
    current = jnp.sqrt(lax.optimization_barrier(jnp.sum(moved * moved, axis=-1, keepdims=True)) + 1e-06)
    return (moved * (target / current)).astype(jnp.bfloat16)

def apply_fast(query_rows, gate, upward, downward):
    gate_pre = jnp.dot(query_rows, gate.T, preferred_element_type=jnp.float32)
    up_pre = jnp.dot(query_rows, upward.T, preferred_element_type=jnp.float32)
    activated, slope = silu_parts(gate_pre)
    applied = (activated * up_pre).astype(jnp.bfloat16)
    return jnp.dot(applied, downward.T, preferred_element_type=jnp.float32)

def window_attention(queries, keys, values):
    width = queries.shape[1]
    span = WINDOW - 1
    scale = ATT_DIM ** (-0.5)
    padding = jnp.zeros((span, width), jnp.bfloat16)
    padded_keys = jnp.concatenate([padding, keys], axis=0)
    padded_values = jnp.concatenate([padding, values], axis=0)
    length = TOK_DEV + span
    row_ids = jnp.arange(TOK_DEV, dtype=jnp.int32)[:, None]
    col_ids = jnp.arange(length, dtype=jnp.int32)[None, :]

    def one_block(block_index):
        start = (block_index * TOK_DEV).astype(jnp.int32)
        query_block = lax.dynamic_slice_in_dim(queries, start, TOK_DEV, 0).astype(jnp.float32)
        key_block = lax.dynamic_slice_in_dim(padded_keys, start, length, 0).astype(jnp.float32)
        value_block = lax.dynamic_slice_in_dim(padded_values, start, length, 0).astype(jnp.float32)
        query_heads = query_block.reshape(TOK_DEV, ATT_HEADS, ATT_DIM)
        key_heads = key_block.reshape(length, ATT_HEADS, ATT_DIM)
        value_heads = value_block.reshape(length, ATT_HEADS, ATT_DIM)
        scores = jnp.einsum('thd,shd->hts', query_heads, key_heads) * scale
        valid = (col_ids >= row_ids) & (col_ids <= row_ids + span) & (col_ids >= span - start)
        scores = jnp.where(valid[None], scores, -1e+30)
        highest = lax.optimization_barrier(jnp.max(scores, axis=-1, keepdims=True))
        weights = jnp.exp(scores - highest)
        probs = (weights / lax.optimization_barrier(jnp.sum(weights, axis=-1, keepdims=True))).astype(jnp.bfloat16)
        output = jnp.einsum('hts,shd->thd', probs.astype(jnp.float32), value_heads)
        return output.reshape(TOK_DEV, width)
    blocks = queries.shape[0] // TOK_DEV
    outputs = lax.map(one_block, jnp.arange(blocks, dtype=jnp.int32))
    return outputs.reshape(queries.shape[0], width)

def reference(queries, keys, values, rates, fast_gate, fast_up, fast_down):
    attended = window_attention(queries, keys, values)
    pieces = []
    for head_index in range(FAST_HEADS):
        first = head_index * FAST_DIM
        last = first + FAST_DIM
        gradient = fast_gradients(keys[:, first:last], values[:, first:last], rates[:, head_index], fast_gate[head_index], fast_up[head_index], fast_down[head_index])
        stacked = jnp.stack([fast_gate[head_index], fast_up[head_index], fast_down[head_index]])
        fresh = renormalize(stacked.reshape(3 * FAST_DIM, FAST_DIM), gradient.reshape(3 * FAST_DIM, FAST_DIM))
        fresh = fresh.reshape(3, FAST_DIM, FAST_DIM)
        pieces.append(apply_fast(queries[:, first:last], fresh[0], fresh[1], fresh[2]))
    trained = jnp.concatenate(pieces, axis=1)
    return (attended + trained).astype(jnp.bfloat16)
```

```python
import functools
import math

import jax
import jax.numpy as jnp
from jax import lax
from jax.experimental import pallas as pl
from jax.experimental.pallas import tpu as pltpu
from jax.sharding import PartitionSpec as P

ATT_DIM = 128
FAST_DIM = 512
WINDOW = 1024
F32 = jnp.float32
BF16 = jnp.bfloat16
COEF = math.log2(math.e) / math.sqrt(ATT_DIM)


def dot_nt(a, b):
    return lax.dot_general(a, b, (((1,), (1,)), ((), ())), preferred_element_type=F32)


def dot_tn(a, b):
    return lax.dot_general(a, b, (((0,), (0,)), ((), ())), preferred_element_type=F32)


def dot_nn(a, b):
    return lax.dot_general(a, b, (((1,), (0,)), ((), ())), preferred_element_type=F32)


def kernel(
    n, orders, q_hbm, k_hbm, v_hbm, rates_ref, gate_hbm, up_hbm, down_hbm, out_ref,
    kwin, vwin, qbuf, wbuf, gsend, grecv, acc, sbuf, rbuf, fresh, lse, oacc,
    load_sem, kv_send, kv_recv, core_send, core_recv,
    rs_send, rs_recv, ag_send, ag_recv, fw_send, fw_recv,
):
    me = lax.axis_index("ctx")
    tok = qbuf.shape[0]
    halo = WINDOW
    tail = halo - 2 * tok
    heads = qbuf.shape[1] // ATT_DIM
    rows = acc.shape[1]
    steps = len(orders[0])
    core = lax.rem(me, 2)
    sibling = me + 1 - 2 * core

    def bit_of(b):
        return lax.rem(lax.div(me, 1 << b), 2)

    def partner(b):
        return me + (1 - 2 * bit_of(b)) * (1 << b)

    own = pl.ds(halo, tok)
    loads = [
        pltpu.make_async_copy(k_hbm, kwin.at[own], load_sem.at[0]),
        pltpu.make_async_copy(v_hbm, vwin.at[own], load_sem.at[1]),
        pltpu.make_async_copy(gate_hbm, wbuf.at[:, pl.ds(0 * FAST_DIM, FAST_DIM)], load_sem.at[2]),
        pltpu.make_async_copy(up_hbm, wbuf.at[:, pl.ds(1 * FAST_DIM, FAST_DIM)], load_sem.at[3]),
        pltpu.make_async_copy(down_hbm, wbuf.at[:, pl.ds(2 * FAST_DIM, FAST_DIM)], load_sem.at[4]),
        pltpu.make_async_copy(q_hbm, qbuf, load_sem.at[5]),
    ]
    for load in loads:
        load.start()

    barrier = pltpu.get_barrier_semaphore()
    greeted = [partner(b) for b in range(steps + 1)]
    for shift in (2, n - 2, 3, n - 3):
        greeted.append(lax.rem(me + shift, n))
    for other in greeted:
        pl.semaphore_signal(
            barrier, inc=1, device_id={"ctx": other}, device_id_type=pl.DeviceIdType.MESH
        )
    pl.semaphore_wait(barrier, len(greeted))

    def remote(src, dst, send, recv, to):
        return pltpu.make_async_remote_copy(
            src_ref=src, dst_ref=dst, send_sem=send, recv_sem=recv,
            device_id={"ctx": to}, device_id_type=pl.DeviceIdType.MESH,
        )

    last = pl.ds(halo + tok - tail, tail)
    far = pl.ds(0, tail)
    mid = pl.ds(tail, tok)
    near = pl.ds(tail + tok, tok)

    def pair(src, dst, lane, to):
        return [
            remote(win.at[src], win.at[dst], kv_send.at[lane, w], kv_recv.at[lane, w], to)
            for w, win in enumerate((kwin, vwin))
        ]

    two = pair(own, mid, 0, lax.rem(me + 2, n))
    near_own = pair(own, near, 1, sibling)
    three = pair(last, far, 2, lax.rem(me + 3, n))
    near_pass = pair(mid, near, 1, sibling)
    far_pass = pair(pl.ds(tail + tok - tail, tail), far, 2, sibling)

    loads[0].wait()
    loads[1].wait()

    def begin(copies):
        for copy in copies:
            copy.start()

    @pl.when(me + 2 < n)
    def _():
        begin(two)

    @pl.when(core == 0)
    def _():
        begin(near_own)

    @pl.when((core == 1) & (me + 3 < n))
    def _():
        begin(three)

    zero_far = jnp.zeros((tail, kwin.shape[1]), BF16)
    zero_tok = jnp.zeros((tok, kwin.shape[1]), BF16)

    @pl.when(me < 3)
    def _():
        kwin[far] = zero_far
        vwin[far] = zero_far

    @pl.when(me < 2)
    def _():
        kwin[mid] = zero_tok
        vwin[mid] = zero_tok

    @pl.when(me < 1)
    def _():
        kwin[near] = zero_tok
        vwin[near] = zero_tok

    for load in loads[2:5]:
        load.wait()

    lane_ids = lax.broadcasted_iota(jnp.int32, rates_ref.shape, 1)

    def gradients(head, store):
        cols = pl.ds(pl.multiple_of(head * FAST_DIM, FAST_DIM), FAST_DIM)
        keys = kwin[own, cols]
        rate = jnp.sum(
            jnp.where(lane_ids == head, rates_ref[...].astype(F32), 0.0), axis=1, keepdims=True
        )
        out_grad = (-rate * vwin[own, cols].astype(F32)).astype(BF16)
        gate_pre = dot_nt(keys, wbuf[head, pl.ds(0 * FAST_DIM, FAST_DIM), :])
        up_pre = dot_nt(keys, wbuf[head, pl.ds(1 * FAST_DIM, FAST_DIM), :])
        sig = jax.nn.sigmoid(gate_pre)
        act = gate_pre * sig
        hidden = (act * up_pre).astype(BF16)
        hidden_grad = dot_nn(out_grad, wbuf[head, pl.ds(2 * FAST_DIM, FAST_DIM), :])
        gate_grad = (hidden_grad * up_pre * (sig * (1.0 + gate_pre * (1.0 - sig)))).astype(BF16)
        up_grad = (hidden_grad * act).astype(BF16)
        store(0, dot_tn(gate_grad, keys))
        store(1, dot_tn(up_grad, keys))
        store(2, dot_tn(out_grad, hidden))

    core_copies = [
        remote(gsend.at[j], grecv.at[j], core_send.at[j], core_recv.at[j], sibling)
        for j in range(2)
    ]
    for j in range(2):

        def store_send(m, value, j=j):
            gsend[j, pl.ds(m * FAST_DIM, FAST_DIM), :] = value.astype(BF16)

        gradients((1 - core) * 2 + j, store_send)
        core_copies[j].start()

    start = [jnp.int32(0), jnp.int32(0)]
    spans = [[], []]
    rs_copies = [[], []]

    def slot(k):
        return rows - (rows >> k)

    def halve(j, k):
        size = rows >> k
        half = size // 2
        b = orders[j][k]
        bit = bit_of(b)
        pending = grecv.at[j] if k == 0 else rbuf.at[j, pl.ds(slot(k - 1), size)]
        base = start[j]
        spans[j].append((base, size))

        def at(ref, first):
            return ref[pl.ds(pl.multiple_of(first, 16), half), :]

        give = (1 - bit) * half
        keep = bit * half
        acc_j = acc.at[j]
        place = pl.ds(slot(k), half)
        sbuf[j, place, :] = (at(acc_j, base + give) + at(pending, give).astype(F32)).astype(BF16)
        copy = remote(
            sbuf.at[j, place], rbuf.at[j, place], rs_send.at[j, k], rs_recv.at[j, k], partner(b)
        )
        copy.start()
        rs_copies[j].append(copy)
        acc[j, pl.ds(pl.multiple_of(base + keep, 16), half), :] = at(acc_j, base + keep) + at(
            pending, keep
        ).astype(F32)
        start[j] = base + keep

    for j in range(2):

        def store_acc(m, value, j=j):
            acc[j, pl.ds(m * FAST_DIM, FAST_DIM), :] = value

        gradients(core * 2 + j, store_acc)
        core_copies[j].wait()
        halve(j, 0)

    loads[5].wait()

    row_ids = lax.broadcasted_iota(jnp.int32, (tok, tok), 0)
    col_ids = lax.broadcasted_iota(jnp.int32, (tok, tok), 1)

    def own_block(a, carry):
        cols = pl.ds(pl.multiple_of(a * ATT_DIM, ATT_DIM), ATT_DIM)
        scores = dot_nt(qbuf[:, cols], kwin[own, cols]) * COEF
        scores = jnp.where(col_ids <= row_ids, scores, -1e30)
        top = jnp.max(scores, axis=1, keepdims=True)
        probs = jnp.exp2(scores - top)
        total = jnp.sum(probs, axis=1, keepdims=True)
        oacc[:, cols] = dot_nn(probs.astype(BF16), vwin[own, cols]) / total
        lse[a] = jnp.broadcast_to(top + jnp.log2(total), (tok, ATT_DIM))
        return carry

    first_key = halo - me * tok
    past = lax.broadcasted_iota(jnp.int32, (1, halo), 1)
    bias = jnp.where(past >= first_key, 0.0, -1e30).astype(F32)

    def halo_block(a, carry):
        cols = pl.ds(pl.multiple_of(a * ATT_DIM, ATT_DIM), ATT_DIM)
        q = qbuf[:, cols]
        edge = dot_nt(q, kwin[pl.ds(0, tok), cols]) * COEF + bias[:, :tok]
        edge = jnp.where(col_ids > row_ids, edge, -1e30)
        rest = dot_nt(q, kwin[pl.ds(tok, halo - tok), cols]) * COEF + bias[:, tok:]
        before = lse[a][:, :1]
        top = jnp.maximum(
            jnp.maximum(jnp.max(edge, axis=1, keepdims=True), jnp.max(rest, axis=1, keepdims=True)),
            before,
        )
        p_edge = jnp.exp2(edge - top)
        p_rest = jnp.exp2(rest - top)
        kept = jnp.exp2(before - top)
        total = (
            kept + jnp.sum(p_edge, axis=1, keepdims=True) + jnp.sum(p_rest, axis=1, keepdims=True)
        )
        mixed = dot_nn(p_edge.astype(BF16), vwin[pl.ds(0, tok), cols]) + dot_nn(
            p_rest.astype(BF16), vwin[pl.ds(tok, halo - tok), cols]
        )
        oacc[:, cols] = (mixed + kept * oacc[:, cols]) / total
        return carry

    cuts = [heads * i // steps for i in range(steps + 1)]
    for k in range(steps):
        lax.fori_loop(cuts[k], cuts[k + 1], own_block, 0)
        if k == 0:
            @pl.when(me >= 2)
            def _():
                for copy in two:
                    copy.wait_recv()

            @pl.when((me >= 2) & (core == 1))
            def _():
                begin(near_pass)

            @pl.when((me >= 2) & (core == 0))
            def _():
                begin(far_pass)

        for j in range(2):
            rs_copies[j][k].wait()
            if k + 1 < steps:
                halve(j, k + 1)

    size = rows >> steps
    ag_copies = [[], []]
    fw_copies = [[], []]

    def forward(j, first, length, index):
        place = pl.ds(pl.multiple_of(first, 16), length)
        copy = remote(
            fresh.at[core * 2 + j, place], fresh.at[core * 2 + j, place],
            fw_send.at[j, index], fw_recv.at[j, index], sibling,
        )
        copy.start()
        arrive = remote(
            fresh.at[core * 2 + j, place], fresh.at[(1 - core) * 2 + j, place],
            fw_send.at[j, index], fw_recv.at[j, index], sibling,
        )
        fw_copies[j].append((copy, arrive))

    def gather(j, k):
        base, length = spans[j][k + 1] if k + 1 < steps else (start[j], size)
        place = pl.ds(pl.multiple_of(base, 16), length)
        copy = remote(
            fresh.at[core * 2 + j, place], fresh.at[core * 2 + j, place],
            ag_send.at[j, k], ag_recv.at[j, k], partner(orders[j][k]),
        )
        copy.start()
        parent = spans[j][k][0]
        incoming = parent + parent + length - base
        arrive = remote(
            fresh.at[core * 2 + j, place],
            fresh.at[core * 2 + j, pl.ds(pl.multiple_of(incoming, 16), length)],
            ag_send.at[j, k], ag_recv.at[j, k], partner(orders[j][k]),
        )
        ag_copies[j].append((copy, arrive, incoming, length))

    for j in range(2):
        place = pl.ds(pl.multiple_of(start[j], 16), size)
        grad = acc[j, place, :] + rbuf[j, pl.ds(slot(steps - 1), size), :].astype(F32)
        initial = wbuf[core * 2 + j, place, :].astype(F32)
        moved = initial - grad
        target = jnp.sqrt(jnp.sum(initial * initial, axis=1, keepdims=True))
        current = jnp.sqrt(jnp.sum(moved * moved, axis=1, keepdims=True) + 1e-06)
        fresh[core * 2 + j, place, :] = (moved * (target / current)).astype(BF16)
        gather(j, steps - 1)
        forward(j, start[j], size, 0)

    @pl.when(me >= 1)
    def _():
        for copy in near_own:
            copy.wait_recv()

    @pl.when(me >= 3)
    def _():
        for copy in three:
            copy.wait_recv()

    cuts = [heads * i // steps for i in range(steps + 1)]
    for i in range(steps):
        lax.fori_loop(cuts[i], cuts[i + 1], halo_block, 0)
        k = steps - 1 - i
        for j in range(2):
            copy, arrive, incoming, length = ag_copies[j][i]
            arrive.wait_recv()
            if k > 0:
                gather(j, k - 1)
            forward(j, incoming, length, i + 1)

    def apply(head):
        cols = pl.ds(pl.multiple_of(head * FAST_DIM, FAST_DIM), FAST_DIM)
        q = qbuf[:, cols]
        gate_pre = dot_nt(q, fresh[head, pl.ds(0, FAST_DIM), :])
        up_pre = dot_nt(q, fresh[head, pl.ds(FAST_DIM, FAST_DIM), :])
        applied = (gate_pre * jax.nn.sigmoid(gate_pre) * up_pre).astype(BF16)
        trained = dot_nt(applied, fresh[head, pl.ds(2 * FAST_DIM, FAST_DIM), :])
        out_ref[:, cols] = (oacc[:, cols] + trained).astype(BF16)

    for j in range(2):
        apply(core * 2 + j)
    for j in range(2):
        for copy, arrive in fw_copies[j]:
            arrive.wait_recv()
        apply((1 - core) * 2 + j)

    for j in range(2):
        for copy, arrive, incoming, length in ag_copies[j]:
            copy.wait_send()
        for copy, arrive in fw_copies[j]:
            copy.wait_send()

    def drain(copies):
        for copy in copies:
            copy.wait_send()

    @pl.when(me + 2 < n)
    def _():
        drain(two)

    @pl.when(core == 0)
    def _():
        drain(near_own)

    @pl.when((core == 1) & (me + 3 < n))
    def _():
        drain(three)

    @pl.when((me >= 2) & (core == 1))
    def _():
        drain(near_pass)

    @pl.when((me >= 2) & (core == 0))
    def _():
        drain(far_pass)


def local(n, orders, queries, keys, values, rates, fast_gate, fast_up, fast_down):
    tok, width = queries.shape
    group = fast_gate.shape[0]
    rows = 3 * FAST_DIM
    steps = len(orders[0])
    dma = pltpu.SemaphoreType.DMA
    hbm = pl.BlockSpec(memory_space=pl.ANY)
    vmem = pl.BlockSpec(memory_space=pltpu.VMEM)
    return pl.pallas_call(
        functools.partial(kernel, n, orders),
        out_shape=jax.ShapeDtypeStruct((tok, width), BF16),
        in_specs=[hbm, hbm, hbm, vmem, hbm, hbm, hbm],
        out_specs=vmem,
        scratch_shapes=[
            pltpu.VMEM((WINDOW + tok, width), BF16),
            pltpu.VMEM((WINDOW + tok, width), BF16),
            pltpu.VMEM((tok, width), BF16),
            pltpu.VMEM((group, rows, FAST_DIM), BF16),
            pltpu.VMEM((2, rows, FAST_DIM), BF16),
            pltpu.VMEM((2, rows, FAST_DIM), BF16),
            pltpu.VMEM((2, rows, FAST_DIM), F32),
            pltpu.VMEM((2, rows, FAST_DIM), BF16),
            pltpu.VMEM((2, rows, FAST_DIM), BF16),
            pltpu.VMEM((group, rows, FAST_DIM), BF16),
            pltpu.VMEM((width // ATT_DIM, tok, ATT_DIM), F32),
            pltpu.VMEM((tok, width), F32),
            dma((6,)),
            dma((3, 2)),
            dma((3, 2)),
            dma((2,)),
            dma((2,)),
            dma((2, steps)),
            dma((2, steps)),
            dma((2, steps)),
            dma((2, steps)),
            dma((2, steps + 1)),
            dma((2, steps + 1)),
        ],
        compiler_params=pltpu.CompilerParams(
            collective_id=0, has_side_effects=True, vmem_limit_bytes=63 * 1024 * 1024
        ),
        cost_estimate=pl.CostEstimate(
            flops=12_000_000_000, bytes_accessed=14_000_000, transcendentals=10_000_000
        ),
    )(queries, keys, values, rates, fast_gate, fast_up, fast_down)


def solution(mesh):
    n = mesh.shape["ctx"]
    bits = n.bit_length() - 1
    order = list(range(1, bits))
    orders = (tuple(order), tuple(order[1:2] + order[:1] + order[2:]))
    in_specs = (P("ctx", "head"),) * 4 + (P("head", None, None),) * 3
    return jax.shard_map(
        functools.partial(local, n, orders),
        mesh=mesh,
        in_specs=in_specs,
        out_specs=P("ctx", "head"),
        check_vma=False,
    )
```
